256 devices in a mesh: ctx: 32 (over y_hi, z, core), tp: 8 (over x, y_lo).
Axes of the slice: x: 4, y: 4 (y_hi: 2, y_lo: 2; y = y_hi * 2 + y_lo), z: 8, core: 2. Of those that a mesh axis runs over, the one named last changes fastest.
Arguments:
- qkv: bfloat16 [3, 4096, 4096], P(None, 'tp', 'ctx'), may hold values from -6 to 6
- short_w: float32 [3, 3, 4096], P(None, None, ('tp', 'ctx')), may hold values from -1 to 1
- filters: float32 [4096, 4096], P(('tp', 'ctx')), may hold values from -0.09375 to 0.09375
- skip: float32 [4096], P(('tp', 'ctx')), may hold values from -4 to 4
- w_out: bfloat16 [4096, 4096], P('tp', 'ctx'), may hold values from -0.09375 to 0.09375
- grad_out: bfloat16 [4096, 4096], P('ctx', 'tp'), may hold values from -6 to 6
Outputs:
- output: bfloat16 [4096, 4096], P('ctx', 'tp')
- grad_qkv: bfloat16 [3, 4096, 4096], P(None, 'tp', 'ctx')
- grad_filters: float32 [4096, 4096], P(('tp', 'ctx'))
- grad_w_out: float32 [4096, 4096], P('tp', 'ctx')
The draws below stay inside these ranges and needn't reach their ends.
All inputs are finite; a program needn't handle non-finite values.
Results may differ from the reference program's by a relative error of at most 0.02.
Values may be sent and summed in bfloat16 or wider, within the bound.
No kernel may reach another device: no remote copies, remote signals or barrier semaphores. Data moves between devices by JAX's collectives and lax.ppermute only.
A program may use at most 64 MiB of HBM per device.

```python
import jax
import jax.numpy as jnp
from jax import lax

C = 4096
DO = 4096
SEQ = 4096


def with_spikes(values, own_key, source, target, parts, factor):
    def block_of(axis_at):
        return (jnp.arange(values.shape[axis_at]) // (values.shape[axis_at] // parts)).reshape((-1,) + (1,) * (values.ndim - 1 - axis_at))

    one_side = jax.random.permutation(own_key, parts)[block_of(target)]
    second = (block_of(target) + parts // 2) % parts
    return jnp.where((block_of(source) == one_side) | (block_of(source) == second), factor * values, values)


def steps_of(key, extent, shards, low, largest):
    def one(dim, blocks):
        heights = jax.random.uniform(jax.random.fold_in(jax.random.fold_in(key, 6), dim), (blocks,), jnp.float32, low / len(shards), largest / len(shards))
        return jnp.repeat(jnp.exp(heights), extent[dim] // blocks).reshape((-1,) + (1,) * (len(extent) - dim - 1))

    level = one(*shards[0])
    for cut in shards[1:]:
        level = level * one(*cut)
    return level


def centred(stream_key, shape, deviation, most, split=(), kind=jnp.bfloat16):
    values = deviation * jax.random.normal(stream_key, shape, jnp.float32)
    if split:
        values = values * steps_of(stream_key, shape, split, -0.22, 0.18)
    return jnp.clip(values, -most, most).astype(kind)


def gaussian_with(own_key, shape, deviation, bound, shards, heavy, held_as=jnp.bfloat16):
    entries = deviation * jax.random.normal(own_key, shape, jnp.float32)
    if shards:
        entries = entries * steps_of(own_key, shape, shards, -0.22, 0.18)
    return jnp.clip(with_spikes(entries, jax.random.fold_in(own_key, 3), *heavy), -bound, bound).astype(held_as)


def setup_inputs(seed: int = 0) -> dict:
    seeds = jax.random.split(jax.random.key(seed), 7)
    return {
        "qkv": centred(seeds[0], (3, C, SEQ), 1.0, 6.0, ((1, 8), (2, 32))),
        "short_w": jnp.clip(jax.random.uniform(seeds[1], (3, 3, C), jnp.float32, -1.0, 1.0) * steps_of(seeds[1], (3, 3, C), ((2, 256),), -0.4, 0.0), -1.0, 1.0),
        "filters": centred(seeds[2], (C, SEQ), SEQ ** -0.5, 0.09375, ((0, 256),), jnp.float32),
        "skip": centred(seeds[3], (C,), 1.0, 4.0, ((0, 256),), jnp.float32),
        "w_out": centred(seeds[4], (C, DO), C ** -0.5, 0.09375, ((0, 8), (1, 32))),
        "grad_out": gaussian_with(seeds[5], (SEQ, DO), 1.0, 6.0, ((0, 32), (1, 8)), (0, 1, 32, 2.75)),
    }


def shift_right(values, steps):
    length = values.shape[-1]
    padded = jnp.pad(values, [(0, 0)] * (values.ndim - 1) + [(steps, 0)])
    return padded[..., :length]


def shift_left(values, steps):
    padded = jnp.pad(values, [(0, 0)] * (values.ndim - 1) + [(0, steps)])
    return padded[..., steps:]


def short_forward(values, weights):
    result = weights[:, 0, :, None] * values
    result = result + weights[:, 1, :, None] * shift_right(values, 1)
    result = result + weights[:, 2, :, None] * shift_right(values, 2)
    return result


def short_backward(grads, weights):
    result = weights[:, 0, :, None] * grads
    result = result + weights[:, 1, :, None] * shift_left(grads, 1)
    result = result + weights[:, 2, :, None] * shift_left(grads, 2)
    return result


def causal_conv(kernel, signal):
    length = signal.shape[-1]
    spectrum = jnp.fft.rfft(kernel, 2 * length) * jnp.fft.rfft(signal, 2 * length)
    return jnp.fft.irfft(spectrum, 2 * length)[..., :length]


def correlate(first, second):
    length = second.shape[-1]
    spectrum = jnp.conj(jnp.fft.rfft(first, 2 * length)) * jnp.fft.rfft(second, 2 * length)
    return jnp.fft.irfft(spectrum, 2 * length)[..., :length]


def mixer_parts(stream, weight, kernel, gain):
    conv = short_forward(stream.astype(jnp.float32), weight)
    query = conv[0].astype(jnp.bfloat16)
    gated = (conv[1] * conv[2]).astype(jnp.bfloat16)
    query_f = lax.optimization_barrier(query).astype(jnp.float32)
    gated_f = lax.optimization_barrier(gated).astype(jnp.float32)
    signal = causal_conv(kernel, gated_f) + gain[:, None] * gated_f
    return conv, query_f, gated_f, signal


def reference(qkv, short_w, filters, skip, w_out, grad_out):
    channels = qkv.shape[1]
    block = min(channels, 256)
    count = channels // block
    streams = qkv.reshape(3, count, block, -1).transpose(1, 0, 2, 3)
    weights = short_w.reshape(3, 3, count, block).transpose(2, 0, 1, 3)
    kernels = filters.reshape(count, block, -1)
    gains = skip.reshape(count, block)
    scale = SEQ ** -0.5

    def forward_block(items):
        stream, weight, kernel, gain = items
        conv, query_f, gated_f, signal = mixer_parts(stream, weight, kernel, gain)
        return (query_f * signal).astype(jnp.bfloat16)

    mixed = lax.map(forward_block, (streams, weights, kernels, gains)).reshape(channels, -1)
    output = jnp.dot(mixed.T, w_out, preferred_element_type=jnp.float32).astype(jnp.bfloat16)
    grad_mixed = jnp.dot(w_out, grad_out.T, preferred_element_type=jnp.float32).astype(jnp.bfloat16)
    grad_w_out = jnp.dot(mixed, grad_out, preferred_element_type=jnp.float32) * scale

    def backward_block(items):
        stream, weight, kernel, gain, upstream = items
        conv, query_f, gated_f, signal = mixer_parts(stream, weight, kernel, gain)
        upstream_f = lax.optimization_barrier(upstream).astype(jnp.float32)
        grad_signal = upstream_f * query_f
        grad_query = (upstream_f * signal).astype(jnp.bfloat16)
        grad_gated = (correlate(kernel, grad_signal) + gain[:, None] * grad_signal).astype(jnp.bfloat16)
        grad_kernel = correlate(gated_f, grad_signal) * scale
        query_back = lax.optimization_barrier(grad_query).astype(jnp.float32)
        gated_back = lax.optimization_barrier(grad_gated).astype(jnp.float32)
        stacked = jnp.stack([query_back, gated_back * conv[2], gated_back * conv[1]])
        return short_backward(stacked, weight).astype(jnp.bfloat16), grad_kernel

    grads, grad_kernels = lax.map(backward_block, (streams, weights, kernels, gains, grad_mixed.reshape(count, block, -1)))
    grad_qkv = grads.transpose(1, 0, 2, 3).reshape(3, channels, -1)
    return output, grad_qkv, grad_kernels.reshape(channels, -1), grad_w_out
```

```python
import functools
import math

import jax
import jax.numpy as jnp
import ml_dtypes
import numpy as np
from jax import lax
from jax.experimental import pallas as pl
from jax.experimental.pallas import tpu as pltpu
from jax.sharding import PartitionSpec as P

F32 = jnp.float32
BF16 = jnp.bfloat16
SEQ = 4096
CH = 16
SH = 32
LN = 128
HALF = 40
VM = pl.BlockSpec(memory_space=pltpu.VMEM)
SM = pl.BlockSpec(memory_space=pltpu.SMEM)
PARAMS = pltpu.CompilerParams(vmem_limit_bytes=48 * 1024 * 1024)


def split(table):
    high = table.astype(ml_dtypes.bfloat16)
    low = (table - high.astype(np.float64)).astype(ml_dtypes.bfloat16)
    return np.stack([high, low])


def tables():
    d = np.arange(HALF)[:, None]
    live = d <= 32
    a = np.arange(SH)[None, :]
    b = np.arange(LN)
    one = 2 * math.pi * d * a / 64
    first = np.concatenate([np.cos(one) * live, -np.sin(one) * live], axis=0)
    turn = 2 * math.pi * d * b[None, :] / 8192
    twist = np.stack([np.cos(turn), np.sin(turn)]).astype(np.float32)
    two = 2 * math.pi * b[:, None] * b[None, :] / 128
    c2, s2 = np.cos(two), np.sin(two)
    second = np.block([[c2, -s2], [s2, c2]])
    back = np.block([[c2, s2], [-s2, c2]])
    weight = np.where((d == 0) | (d == 32), 1.0, 2.0) * live / 8192
    last = np.concatenate([(np.cos(one) * weight).T, (-np.sin(one) * weight).T], axis=1)
    return split(first), twist, split(second), split(back), split(last)


def parts(values):
    high = values.astype(BF16)
    low = (values - high.astype(F32)).astype(BF16)
    return high, low


def dot(left, right):
    return lax.dot_general(left, right, (((1,), (0,)), ((), ())), preferred_element_type=F32)


def table_left(table, values):
    high, low = parts(values)
    return dot(table[0], high) + dot(table[0], low) + dot(table[1], high)


def table_right(values, table):
    high, low = parts(values)
    return dot(high, table[0]) + dot(low, table[0]) + dot(high, table[1])


def column(c):
    return slice(c * LN, (c + 1) * LN)


def forward(values, first, twist, second, work):
    grid = table_left(first, values)
    cosine, sine = twist[0], twist[1]
    for c in range(CH):
        real, imag = grid[:HALF, column(c)], grid[HALF:, column(c)]
        work[c * HALF : (c + 1) * HALF, :LN] = real * cosine + imag * sine
        work[c * HALF : (c + 1) * HALF, LN:] = imag * cosine - real * sine
    return table_right(work[...], second)


def inverse(spectrum, twist, back, last):
    grid = table_right(spectrum, back)
    cosine, sine = twist[0], twist[1]
    columns = []
    for c in range(CH):
        real = grid[c * HALF : (c + 1) * HALF, :LN]
        imag = grid[c * HALF : (c + 1) * HALF, LN:]
        columns.append(
            jnp.concatenate([real * cosine - imag * sine, imag * cosine + real * sine], axis=0)
        )
    return table_left(last, jnp.concatenate(columns, axis=1))


def times(first, second, conjugate):
    ar, ai = first[:, :LN], first[:, LN:]
    br, bi = second[:, :LN], second[:, LN:]
    if conjugate:
        return jnp.concatenate([ar * br + ai * bi, ar * bi - ai * br], axis=1)
    return jnp.concatenate([ar * br - ai * bi, ar * bi + ai * br], axis=1)


def lane_row():
    lane = lax.broadcasted_iota(jnp.int32, (SH, LN), 1)
    row = lax.broadcasted_iota(jnp.int32, (SH, LN), 0)
    return lane, row


def later(values, steps, lane, row):
    here = pltpu.roll(values, steps, 1)
    above = jnp.where(row >= 1, pltpu.roll(here, 1, 0), 0.0)
    return jnp.where(lane >= steps, here, above)


def sooner(values, steps, lane, row):
    here = pltpu.roll(values, LN - steps, 1)
    below = jnp.where(row < SH - 1, pltpu.roll(here, SH - 1, 0), 0.0)
    return jnp.where(lane < LN - steps, here, below)


def filter_kernel(filters, first, twist, second, spectrum, rows, work):
    for a in range(SH):
        rows[pl.ds(a, CH, stride=SH), :] = filters[:, column(a)]
    values = jnp.concatenate([rows[c * SH : (c + 1) * SH, :] for c in range(CH)], axis=1)
    spectrum[...] = forward(values, first, twist, second, work)


def front_kernel(
    streams, short_w, skip, kernel, first, twist, second, back, last,
    outgoing, query, left, right, signal, spectrum, rows, work, packed,
):
    lane, row = lane_row()
    for j in range(SH):
        rows[j * 48 : (j + 1) * 48, :] = streams[j].astype(F32)
    gated = []
    for c in range(CH):
        conv = []
        for s in range(3):
            x = rows[pl.ds(s * CH + c, SH, stride=48), :]
            y = short_w[s, 0, c] * x
            y = y + short_w[s, 1, c] * later(x, 1, lane, row)
            y = y + short_w[s, 2, c] * later(x, 2, lane, row)
            conv.append(y)
        query[:, column(c)] = conv[0].astype(BF16).astype(F32)
        left[:, column(c)] = conv[1]
        right[:, column(c)] = conv[2]
        gated.append((conv[1] * conv[2]).astype(BF16).astype(F32))
    own = forward(jnp.concatenate(gated, axis=1), first, twist, second, work)
    spectrum[...] = own
    total = inverse(times(kernel[...], own, False), twist, back, last)
    for c in range(CH):
        value = total[:, column(c)] + skip[c] * gated[c]
        signal[:, column(c)] = value
        packed[pl.ds(c, SH, stride=CH), :] = query[:, column(c)] * value
    for high in range(2):
        for low in range(4):
            for q in range(4):
                j = high * 16 + q * 4 + low
                piece = packed[j * CH : (j + 1) * CH, :].astype(BF16)
                for target in range(4):
                    outgoing[high * 16 + target * 4 + low, :, column(q)] = piece


def rear_kernel(
    upstream, short_w, skip, kernel, spectrum, query, left, right, signal,
    first, twist, second, back, last,
    outgoing, grad_filters, rows, work, packed, turned,
):
    lane, row = lane_row()
    for high in range(2):
        for low in range(4):
            total = upstream[high * 16 + low].astype(F32)
            for q in range(1, 4):
                total = total + upstream[high * 16 + q * 4 + low].astype(F32)
            for q in range(4):
                j = high * 16 + q * 4 + low
                rows[j * CH : (j + 1) * CH, :] = total[:, column(q)]

    def emit(s, c, x):
        y = short_w[s, 0, c] * x
        y = y + short_w[s, 1, c] * sooner(x, 1, lane, row)
        y = y + short_w[s, 2, c] * sooner(x, 2, lane, row)
        packed[pl.ds(s * CH + c, SH, stride=48), :] = y

    grad_signal = []
    for c in range(CH):
        up = rows[pl.ds(c, SH, stride=CH), :]
        grad_signal.append(up * query[:, column(c)])
        emit(0, c, (up * signal[:, column(c)]).astype(BF16).astype(F32))
    own = forward(jnp.concatenate(grad_signal, axis=1), first, twist, second, work)
    through = inverse(times(kernel[...], own, True), twist, back, last)
    for c in range(CH):
        grad = (through[:, column(c)] + skip[c] * grad_signal[c]).astype(BF16).astype(F32)
        emit(1, c, grad * right[:, column(c)])
        emit(2, c, grad * left[:, column(c)])
    for j in range(SH):
        outgoing[j] = packed[j * 48 : (j + 1) * 48, :].astype(BF16)
    taps = inverse(times(spectrum[...], own, True), twist, back, last)
    for c in range(CH):
        turned[c * SH : (c + 1) * SH, :] = taps[:, column(c)] * (SEQ**-0.5)
    for a in range(SH):
        grad_filters[:, column(a)] = turned[pl.ds(a, CH, stride=SH), :]


def weight_blocks(place, near, far, weight):
    for flip, blocks in ((0, near), (1, far)):
        for k in range(4):
            high = place[0] ^ (k >> 1)
            low = (place[1] ^ (k & 1)) * 2 + (place[2] ^ flip)
            weight[high, :, pl.ds(pl.multiple_of(low * LN, LN), LN)] = blocks[k]


def token_blocks(place, near, far, grad):
    for flip, blocks in ((0, near), (1, far)):
        for k in range(4):
            high = place[3] ^ (k >> 1)
            low = (place[4] ^ (k & 1)) * 2 + (place[5] ^ flip)
            grad[high, pl.ds(pl.multiple_of(low * LN, LN), LN), :] = blocks[k]


def product(left, right, over):
    return lax.dot_general(left, right, ((over[:1], over[1:]), ((), ())), preferred_element_type=F32)


def mixed_grad_kernel(place, w_near, w_far, g_near, g_far, _, outgoing, weight, grad):
    weight_blocks(place, w_near, w_far, weight)
    token_blocks(place, g_near, g_far, grad)
    for half in range(2):
        rows = slice(half * 256, (half + 1) * 256)
        total = product(weight[0, rows, :], grad[0], (1, 1))
        total = total + product(weight[1, rows, :], grad[1], (1, 1))
        outgoing[half * 16 : (half + 1) * 16] = total.astype(BF16).reshape(16, CH, 512)


def projection_kernel(
    place, mixed, w_near, w_far, g_near, g_far, o_near, o_far, d_near, d_far, weight, grad, held
):
    weight_blocks(place, w_near, w_far, weight)
    token_blocks(place, g_near, g_far, grad)
    rows = mixed[...].reshape(512, 512)
    for high in range(2):
        held[high] = product(rows, weight[high], (0, 0)).astype(BF16)
    for flip, blocks in ((0, o_near), (1, o_far)):
        for k in range(4):
            high = place[3] ^ (k >> 1)
            low = (place[4] ^ (k & 1)) * 2 + (place[5] ^ flip)
            blocks[k] = held[high, pl.ds(pl.multiple_of(low * LN, LN), LN), :]
    for high in range(2):
        held[high] = product(rows, grad[high], (1, 0)).astype(BF16)
    for flip, blocks in ((0, d_near), (1, d_far)):
        for k in range(4):
            high = place[0] ^ (k >> 1)
            low = (place[1] ^ (k & 1)) * 2 + (place[2] ^ flip)
            blocks[k] = held[high, :, pl.ds(pl.multiple_of(low * LN, LN), LN)]


def flat(*shape):
    return jax.ShapeDtypeStruct(shape, F32)


def half(*shape):
    return jax.ShapeDtypeStruct(shape, BF16)


def flip(values, axis, size, mask):
    return lax.ppermute(values, axis, [(i, i ^ mask) for i in range(size)])


def exchange(values):
    pairs = []
    for j in range(32):
        for i in range(8):
            to_j = (j & 0b10011) | ((i & 3) << 2)
            to_i = (i & 4) | ((j >> 2) & 3)
            pairs.append((j * 8 + i, to_j * 8 + to_i))
    return lax.ppermute(values, ("ctx", "tp"), pairs)


def shards(qkv, short_w, filters, skip, w_out, grad_out):
    first, twist, second, back, last = [jnp.asarray(t) for t in tables()]
    j, i = lax.axis_index("ctx"), lax.axis_index("tp")
    place = jnp.stack([j >> 4, (j >> 1) & 1, j & 1, i >> 2, (i >> 1) & 1, i & 1]).astype(jnp.int32)

    w_near = jnp.stack([w_out] + [flip(w_out, "ctx", 32, m) for m in (2, 16, 18)])
    w_far = flip(w_near, "ctx", 32, 1)
    tile = exchange(grad_out)
    g_near = jnp.stack([tile] + [flip(tile, "tp", 8, m) for m in (2, 4, 6)])
    g_far = flip(g_near, "tp", 8, 1)

    sent = qkv.reshape(3, SH, CH, LN).transpose(1, 0, 2, 3).reshape(SH, 3 * CH, LN)
    streams = lax.all_to_all(sent, "ctx", 0, 0)

    kernel = pl.pallas_call(
        filter_kernel,
        out_shape=flat(CH * HALF, 2 * LN),
        in_specs=[VM] * 4,
        out_specs=VM,
        scratch_shapes=[pltpu.VMEM((CH * SH, LN), F32), pltpu.VMEM((CH * HALF, 2 * LN), F32)],
        compiler_params=PARAMS,
        name="filter_spectrum",
    )(filters, first, twist, second)

    buffer, query, left, right, signal, spectrum = pl.pallas_call(
        front_kernel,
        out_shape=[half(SH, 2 * CH, 512)] + [flat(SH, CH * LN)] * 4 + [flat(CH * HALF, 2 * LN)],
        in_specs=[VM, SM, SM] + [VM] * 6,
        out_specs=[pl.BlockSpec((SH, CH, 512), lambda g: (0, 0, 0))] + [VM] * 5,
        scratch_shapes=[
            pltpu.VMEM((SH * 48, LN), F32),
            pltpu.VMEM((CH * HALF, 2 * LN), F32),
            pltpu.VMEM((SH * CH, LN), F32),
        ],
        grid=(1,),
        compiler_params=PARAMS,
        name="front",
    )(streams, short_w, skip, kernel, first, twist, second, back, last)

    buffer = pl.pallas_call(
        mixed_grad_kernel,
        out_shape=half(SH, 2 * CH, 512),
        in_specs=[SM] + [VM] * 4 + [pl.BlockSpec(memory_space=pl.ANY)],
        out_specs=pl.BlockSpec((SH, CH, 512), lambda g: (0, 1, 0)),
        scratch_shapes=[pltpu.VMEM((2, 512, 512), BF16), pltpu.VMEM((2, 512, 512), BF16)],
        input_output_aliases={5: 0},
        grid=(1,),
        compiler_params=PARAMS,
        name="mixed_grad",
    )(place, w_near, w_far, g_near, g_far, buffer)

    joint = lax.all_to_all(buffer, "ctx", 0, 0)

    o_near, o_far, d_near, d_far = pl.pallas_call(
        projection_kernel,
        out_shape=[half(4, LN, 512)] * 2 + [half(4, 512, LN)] * 2,
        in_specs=[SM, pl.BlockSpec((SH, CH, 512), lambda g: (0, 0, 0))] + [VM] * 4,
        out_specs=[VM] * 4,
        scratch_shapes=[pltpu.VMEM((2, 512, 512), BF16)] * 3,
        grid=(1,),
        compiler_params=PARAMS,
        name="projections",
    )(place, joint, w_near, w_far, g_near, g_far)

    o_sum = o_near.astype(F32) + flip(o_far, "tp", 8, 1).astype(F32)
    o_sent = o_sum.astype(BF16)
    o_total = o_sum[0]
    for k in range(1, 4):
        o_total = o_total + flip(o_sent[k], "tp", 8, 2 * k).astype(F32)
    output = exchange(o_total.astype(BF16))

    d_sum = d_near.astype(F32) + flip(d_far, "ctx", 32, 1).astype(F32)
    d_sent = d_sum.astype(BF16)
    d_total = d_sum[0]
    for k, m in ((1, 2), (2, 16), (3, 18)):
        d_total = d_total + flip(d_sent[k], "ctx", 32, m).astype(F32)
    grad_w_out = d_total * (SEQ**-0.5)

    grads, grad_filters = pl.pallas_call(
        rear_kernel,
        out_shape=[half(SH, 3 * CH, LN), flat(CH, SEQ)],
        in_specs=[pl.BlockSpec((SH, CH, 512), lambda g: (0, 1, 0)), SM, SM] + [VM] * 11,
        out_specs=[VM, VM],
        scratch_shapes=[
            pltpu.VMEM((SH * CH, LN), F32),
            pltpu.VMEM((CH * HALF, 2 * LN), F32),
            pltpu.VMEM((SH * 48, LN), F32),
            pltpu.VMEM((CH * SH, LN), F32),
        ],
        grid=(1,),
        compiler_params=PARAMS,
        name="rear",
    )(joint, short_w, skip, kernel, spectrum, query, left, right, signal, first, twist, second, back, last)

    returned = lax.all_to_all(grads, "ctx", 0, 0)
    grad_qkv = returned.reshape(SH, 3, CH, LN).transpose(1, 0, 2, 3).reshape(3, SH * CH, LN)
    return (output, grad_qkv, grad_filters, grad_w_out)


def solution(mesh):
    placed = (
        P(None, "tp", "ctx"),
        P(None, None, ("tp", "ctx")),
        P(("tp", "ctx"), None),
        P(("tp", "ctx")),
        P("tp", "ctx"),
        P("ctx", "tp"),
    )
    return jax.shard_map(
        shards,
        mesh=mesh,
        in_specs=placed,
        out_specs=(P("ctx", "tp"), P(None, "tp", "ctx"), P(("tp", "ctx"), None), P("tp", "ctx")),
        check_vma=False,
    )
```

```python
import functools
import math

import jax
import jax.numpy as jnp
import ml_dtypes
import numpy as np
from jax import lax
from jax.experimental import pallas as pl
from jax.experimental.pallas import tpu as pltpu
from jax.sharding import PartitionSpec as P

F32 = jnp.float32
BF16 = jnp.bfloat16
SEQ = 4096
CH = 16
SH = 32
LN = 128
HALF = 40
VM = pl.BlockSpec(memory_space=pltpu.VMEM)
SM = pl.BlockSpec(memory_space=pltpu.SMEM)
PARAMS = pltpu.CompilerParams(vmem_limit_bytes=48 * 1024 * 1024)


def split(table):
    high = table.astype(ml_dtypes.bfloat16)
    low = (table - high.astype(np.float64)).astype(ml_dtypes.bfloat16)
    return np.stack([high, low])


def tables():
    d = np.arange(HALF)[:, None]
    live = d <= 32
    a = np.arange(SH)[None, :]
    b = np.arange(LN)
    one = 2 * math.pi * d * a / 64
    first = np.concatenate([np.cos(one) * live, -np.sin(one) * live], axis=0)
    turn = 2 * math.pi * d * b[None, :] / 8192
    twist = np.stack([np.cos(turn), np.sin(turn)]).astype(np.float32)
    two = 2 * math.pi * b[:, None] * b[None, :] / 128
    c2, s2 = np.cos(two), np.sin(two)
    second = np.block([[c2, -s2], [s2, c2]])
    weight = np.where((d == 0) | (d == 32), 1.0, 2.0) * live / 8192
    last = np.concatenate([(np.cos(one) * weight).T, (-np.sin(one) * weight).T], axis=1)
    return split(first), twist, split(second), split(last)


def parts(values):
    high = values.astype(BF16)
    low = (values - high.astype(F32)).astype(BF16)
    return high, low


def dot(left, right):
    return lax.dot_general(left, right, (((1,), (0,)), ((), ())), preferred_element_type=F32)


def table_left(table, values):
    high, low = parts(values)
    return dot(table[0], high) + dot(table[0], low) + dot(table[1], high)


def table_right(values, table, side):
    def times_table(piece, k):
        return lax.dot_general(
            piece, table[k], (((1,), (side,)), ((), ())), preferred_element_type=F32
        )

    high, low = parts(values)
    return times_table(high, 0) + times_table(low, 0) + times_table(high, 1)


def column(c):
    return slice(c * LN, (c + 1) * LN)


def forward(values, first, twist, second, work):
    grid = table_left(first, values)
    cosine, sine = twist[0], twist[1]
    for c in range(CH):
        real, imag = grid[:HALF, column(c)], grid[HALF:, column(c)]
        work[c * HALF : (c + 1) * HALF, :LN] = real * cosine + imag * sine
        work[c * HALF : (c + 1) * HALF, LN:] = imag * cosine - real * sine
    return table_right(work[...], second, 0)


def inverse(spectrum, twist, second, last):
    grid = table_right(spectrum, second, 1)
    cosine, sine = twist[0], twist[1]
    columns = []
    for c in range(CH):
        real = grid[c * HALF : (c + 1) * HALF, :LN]
        imag = grid[c * HALF : (c + 1) * HALF, LN:]
        columns.append(
            jnp.concatenate([real * cosine - imag * sine, imag * cosine + real * sine], axis=0)
        )
    return table_left(last, jnp.concatenate(columns, axis=1))


def times(first, second, conjugate):
    ar, ai = first[:, :LN], first[:, LN:]
    br, bi = second[:, :LN], second[:, LN:]
    if conjugate:
        return jnp.concatenate([ar * br + ai * bi, ar * bi - ai * br], axis=1)
    return jnp.concatenate([ar * br - ai * bi, ar * bi + ai * br], axis=1)


def lane_row():
    lane = lax.broadcasted_iota(jnp.int32, (SH, LN), 1)
    row = lax.broadcasted_iota(jnp.int32, (SH, LN), 0)
    return lane, row


def later(values, steps, lane, row):
    here = pltpu.roll(values, steps, 1)
    above = jnp.where(row >= 1, pltpu.roll(here, 1, 0), 0.0)
    return jnp.where(lane >= steps, here, above)


def sooner(values, steps, lane, row):
    here = pltpu.roll(values, LN - steps, 1)
    below = jnp.where(row < SH - 1, pltpu.roll(here, SH - 1, 0), 0.0)
    return jnp.where(lane < LN - steps, here, below)


def filter_kernel(filters, first, twist, second, spectrum, rows, work):
    for a in range(SH):
        rows[pl.ds(a, CH, stride=SH), :] = filters[:, column(a)]
    values = jnp.concatenate([rows[c * SH : (c + 1) * SH, :] for c in range(CH)], axis=1)
    spectrum[...] = forward(values, first, twist, second, work)


def front_kernel(
    streams, short_w, skip, kernel, first, twist, second, last,
    outgoing, query, left, right, signal, spectrum, rows, work, packed,
):
    lane, row = lane_row()
    for j in range(SH):
        rows[j * 48 : (j + 1) * 48, :] = streams[j].astype(F32)
    gated = []
    for c in range(CH):
        conv = []
        for s in range(3):
            x = rows[pl.ds(s * CH + c, SH, stride=48), :]
            y = short_w[s, 0, c] * x
            y = y + short_w[s, 1, c] * later(x, 1, lane, row)
            y = y + short_w[s, 2, c] * later(x, 2, lane, row)
            conv.append(y)
        query[:, column(c)] = conv[0].astype(BF16).astype(F32)
        left[:, column(c)] = conv[1]
        right[:, column(c)] = conv[2]
        gated.append((conv[1] * conv[2]).astype(BF16).astype(F32))
    own = forward(jnp.concatenate(gated, axis=1), first, twist, second, work)
    spectrum[...] = own
    total = inverse(times(kernel[...], own, False), twist, second, last)
    for c in range(CH):
        value = total[:, column(c)] + skip[c] * gated[c]
        signal[:, column(c)] = value
        packed[pl.ds(c, SH, stride=CH), :] = query[:, column(c)] * value
    for high in range(2):
        for low in range(4):
            for q in range(4):
                j = high * 16 + q * 4 + low
                piece = packed[j * CH : (j + 1) * CH, :].astype(BF16)
                for target in range(4):
                    outgoing[high * 16 + target * 4 + low, :, column(q)] = piece


def rear_kernel(
    upstream, short_w, skip, kernel, spectrum, query, left, right, signal,
    first, twist, second, last,
    outgoing, grad_filters, rows, work, packed, turned,
):
    lane, row = lane_row()
    for high in range(2):
        for low in range(4):
            total = upstream[high * 16 + low].astype(F32)
            for q in range(1, 4):
                total = total + upstream[high * 16 + q * 4 + low].astype(F32)
            for q in range(4):
                j = high * 16 + q * 4 + low
                rows[j * CH : (j + 1) * CH, :] = total[:, column(q)]

    def emit(s, c, x):
        y = short_w[s, 0, c] * x
        y = y + short_w[s, 1, c] * sooner(x, 1, lane, row)
        y = y + short_w[s, 2, c] * sooner(x, 2, lane, row)
        packed[pl.ds(s * CH + c, SH, stride=48), :] = y

    grad_signal = []
    for c in range(CH):
        up = rows[pl.ds(c, SH, stride=CH), :]
        grad_signal.append(up * query[:, column(c)])
        emit(0, c, (up * signal[:, column(c)]).astype(BF16).astype(F32))
    own = forward(jnp.concatenate(grad_signal, axis=1), first, twist, second, work)
    through = inverse(times(kernel[...], own, True), twist, second, last)
    for c in range(CH):
        grad = (through[:, column(c)] + skip[c] * grad_signal[c]).astype(BF16).astype(F32)
        emit(1, c, grad * right[:, column(c)])
        emit(2, c, grad * left[:, column(c)])
    for j in range(SH):
        outgoing[j] = packed[j * 48 : (j + 1) * 48, :].astype(BF16)
    taps = inverse(times(spectrum[...], own, True), twist, second, last)
    for c in range(CH):
        turned[c * SH : (c + 1) * SH, :] = taps[:, column(c)] * (SEQ**-0.5)
    for a in range(SH):
        grad_filters[:, column(a)] = turned[pl.ds(a, CH, stride=SH), :]


def weight_blocks(place, near, far, weight):
    for flip, blocks in ((0, near), (1, far)):
        for k in range(4):
            high = place[0] ^ (k >> 1)
            low = (place[1] ^ (k & 1)) * 2 + (place[2] ^ flip)
            weight[high, :, pl.ds(pl.multiple_of(low * LN, LN), LN)] = blocks[k]


def token_blocks(place, near, far, grad):
    for flip, blocks in ((0, near), (1, far)):
        for k in range(4):
            high = place[3] ^ (k >> 1)
            low = (place[4] ^ (k & 1)) * 2 + (place[5] ^ flip)
            grad[high, pl.ds(pl.multiple_of(low * LN, LN), LN), :] = blocks[k]


def product(left, right, over):
    return lax.dot_general(left, right, ((over[:1], over[1:]), ((), ())), preferred_element_type=F32)


def mixed_grad_kernel(place, w_near, w_far, g_near, g_far, _, outgoing, weight, grad):
    weight_blocks(place, w_near, w_far, weight)
    token_blocks(place, g_near, g_far, grad)
    for half in range(2):
        rows = slice(half * 256, (half + 1) * 256)
        total = product(weight[0, rows, :], grad[0], (1, 1))
        total = total + product(weight[1, rows, :], grad[1], (1, 1))
        outgoing[half * 16 : (half + 1) * 16] = total.astype(BF16).reshape(16, CH, 512)


def projection_kernel(
    place, mixed, w_near, w_far, g_near, g_far, o_near, o_far, d_near, d_far, weight, grad, held
):
    weight_blocks(place, w_near, w_far, weight)
    token_blocks(place, g_near, g_far, grad)
    rows = mixed[...].reshape(512, 512)
    for high in range(2):
        held[high] = product(rows, weight[high], (0, 0)).astype(BF16)
    for flip, blocks in ((0, o_near), (1, o_far)):
        for k in range(4):
            high = place[3] ^ (k >> 1)
            low = (place[4] ^ (k & 1)) * 2 + (place[5] ^ flip)
            blocks[k] = held[high, pl.ds(pl.multiple_of(low * LN, LN), LN), :]
    for high in range(2):
        held[high] = product(rows, grad[high], (1, 0)).astype(BF16)
    for flip, blocks in ((0, d_near), (1, d_far)):
        for k in range(4):
            high = place[0] ^ (k >> 1)
            low = (place[1] ^ (k & 1)) * 2 + (place[2] ^ flip)
            blocks[k] = held[high, :, pl.ds(pl.multiple_of(low * LN, LN), LN)]


def flat(*shape):
    return jax.ShapeDtypeStruct(shape, F32)


def half(*shape):
    return jax.ShapeDtypeStruct(shape, BF16)


def flip(values, axis, size, mask):
    return lax.ppermute(values, axis, [(i, i ^ mask) for i in range(size)])


def exchange(values):
    pairs = []
    for j in range(32):
        for i in range(8):
            to_j = (j & 0b10011) | ((i & 3) << 2)
            to_i = (i & 4) | ((j >> 2) & 3)
            pairs.append((j * 8 + i, to_j * 8 + to_i))
    return lax.ppermute(values, ("ctx", "tp"), pairs)


def shards(qkv, short_w, filters, skip, w_out, grad_out):
    first, twist, second, last = [jnp.asarray(t) for t in tables()]
    j, i = lax.axis_index("ctx"), lax.axis_index("tp")
    place = jnp.stack([j >> 4, (j >> 1) & 1, j & 1, i >> 2, (i >> 1) & 1, i & 1]).astype(jnp.int32)

    sent = qkv.reshape(3, SH, CH, LN).transpose(1, 0, 2, 3).reshape(SH, 3 * CH, LN)
    tile = exchange(grad_out)
    w_got = [flip(w_out, "ctx", 32, m) for m in (2, 16, 18)]
    sent, tile, place, *w_got = lax.optimization_barrier((sent, tile, place, *w_got))
    streams = lax.all_to_all(sent, "ctx", 0, 0)
    near = jnp.stack([tile] + [flip(tile, "tp", 8, m) for m in (2, 4, 6)])
    tiles = [near, flip(near, "tp", 8, 1)]
    w_near = jnp.stack([w_out, *w_got])
    streams, _ = lax.optimization_barrier((streams, near))
    w_far = flip(w_near, "ctx", 32, 1)

    kernel = pl.pallas_call(
        filter_kernel,
        out_shape=flat(CH * HALF, 2 * LN),
        in_specs=[VM] * 4,
        out_specs=VM,
        scratch_shapes=[pltpu.VMEM((CH * SH, LN), F32), pltpu.VMEM((CH * HALF, 2 * LN), F32)],
        compiler_params=PARAMS,
        name="filter_spectrum",
    )(filters, first, twist, second)

    buffer, query, left, right, signal, spectrum = pl.pallas_call(
        front_kernel,
        out_shape=[half(SH, 2 * CH, 512)] + [flat(SH, CH * LN)] * 4 + [flat(CH * HALF, 2 * LN)],
        in_specs=[VM, SM, SM] + [VM] * 5,
        out_specs=[pl.BlockSpec((SH, CH, 512), lambda g: (0, 0, 0))] + [VM] * 5,
        scratch_shapes=[
            pltpu.VMEM((SH * 48, LN), F32),
            pltpu.VMEM((CH * HALF, 2 * LN), F32),
            pltpu.VMEM((SH * CH, LN), F32),
        ],
        grid=(1,),
        compiler_params=PARAMS,
        name="front",
    )(streams, short_w, skip, kernel, first, twist, second, last)

    buffer = pl.pallas_call(
        mixed_grad_kernel,
        out_shape=half(SH, 2 * CH, 512),
        in_specs=[SM] + [VM] * 4 + [pl.BlockSpec(memory_space=pl.ANY)],
        out_specs=pl.BlockSpec((SH, CH, 512), lambda g: (0, 1, 0)),
        scratch_shapes=[pltpu.VMEM((2, 512, 512), BF16), pltpu.VMEM((2, 512, 512), BF16)],
        input_output_aliases={5: 0},
        grid=(1,),
        compiler_params=PARAMS,
        name="mixed_grad",
    )(place, w_near, w_far, *tiles, buffer)

    joint = lax.all_to_all(buffer, "ctx", 0, 0)

    o_near, o_far, d_near, d_far = pl.pallas_call(
        projection_kernel,
        out_shape=[half(4, LN, 512)] * 2 + [half(4, 512, LN)] * 2,
        in_specs=[SM, pl.BlockSpec((SH, CH, 512), lambda g: (0, 0, 0))] + [VM] * 4,
        out_specs=[VM] * 4,
        scratch_shapes=[pltpu.VMEM((2, 512, 512), BF16)] * 3,
        grid=(1,),
        compiler_params=PARAMS,
        name="projections",
    )(place, joint, w_near, w_far, *tiles)

    o_sum = o_near.astype(F32) + flip(o_far, "tp", 8, 1).astype(F32)
    o_sent = o_sum.astype(BF16)
    o_total = o_sum[0]
    for k in range(1, 4):
        o_total = o_total + flip(o_sent[k], "tp", 8, 2 * k).astype(F32)
    output = exchange(o_total.astype(BF16))

    d_sum = d_near.astype(F32) + flip(d_far, "ctx", 32, 1).astype(F32)
    d_sent = d_sum.astype(BF16)
    d_total = d_sum[0]
    for k, m in ((1, 2), (2, 16), (3, 18)):
        d_total = d_total + flip(d_sent[k], "ctx", 32, m).astype(F32)
    grad_w_out = d_total * (SEQ**-0.5)

    grads, grad_filters = pl.pallas_call(
        rear_kernel,
        out_shape=[half(SH, 3 * CH, LN), flat(CH, SEQ)],
        in_specs=[pl.BlockSpec((SH, CH, 512), lambda g: (0, 1, 0)), SM, SM] + [VM] * 10,
        out_specs=[VM, VM],
        scratch_shapes=[
            pltpu.VMEM((SH * CH, LN), F32),
            pltpu.VMEM((CH * HALF, 2 * LN), F32),
            pltpu.VMEM((SH * 48, LN), F32),
            pltpu.VMEM((CH * SH, LN), F32),
        ],
        grid=(1,),
        compiler_params=PARAMS,
        name="rear",
    )(joint, short_w, skip, kernel, spectrum, query, left, right, signal, first, twist, second, last)

    returned = lax.all_to_all(grads, "ctx", 0, 0)
    grad_qkv = returned.reshape(SH, 3, CH, LN).transpose(1, 0, 2, 3).reshape(3, SH * CH, LN)
    return (output, grad_qkv, grad_filters, grad_w_out)


def solution(mesh):
    placed = (
        P(None, "tp", "ctx"),
        P(None, None, ("tp", "ctx")),
        P(("tp", "ctx"), None),
        P(("tp", "ctx")),
        P("tp", "ctx"),
        P("ctx", "tp"),
    )
    return jax.shard_map(
        shards,
        mesh=mesh,
        in_specs=placed,
        out_specs=(P("ctx", "tp"), P(None, "tp", "ctx"), P(("tp", "ctx"), None), P("tp", "ctx")),
        check_vma=False,
    )
```

```python
import functools
import math

import jax
import jax.numpy as jnp
import ml_dtypes
import numpy as np
from jax import lax
from jax.experimental import pallas as pl
from jax.experimental.pallas import tpu as pltpu
from jax.sharding import PartitionSpec as P

F32 = jnp.float32
BF16 = jnp.bfloat16
SEQ = 4096
CH = 16
SH = 32
LN = 128
HALF = 40
VM = pl.BlockSpec(memory_space=pltpu.VMEM)
SM = pl.BlockSpec(memory_space=pltpu.SMEM)
PARAMS = pltpu.CompilerParams(vmem_limit_bytes=32 * 1024 * 1024)


def split(table):
    high = table.astype(ml_dtypes.bfloat16)
    low = (table - high.astype(np.float64)).astype(ml_dtypes.bfloat16)
    return np.stack([high, low])


def tables():
    d = np.arange(HALF)[:, None]
    live = d <= 32
    a = np.arange(SH)[None, :]
    b = np.arange(LN)
    one = 2 * math.pi * d * a / 64
    first = np.concatenate([np.cos(one) * live, -np.sin(one) * live], axis=0)
    turn = 2 * math.pi * d * b[None, :] / 8192
    twist = np.stack([np.cos(turn), np.sin(turn)]).astype(np.float32)
    two = 2 * math.pi * b[:, None] * b[None, :] / 128
    c2, s2 = np.cos(two), np.sin(two)
    second = np.block([[c2, -s2], [s2, c2]])
    weight = np.where((d == 0) | (d == 32), 1.0, 2.0) * live / 8192
    last = np.concatenate([(np.cos(one) * weight).T, (-np.sin(one) * weight).T], axis=1)
    return split(first), twist, split(second), split(last)


def parts(values):
    high = values.astype(BF16)
    low = (values - high.astype(F32)).astype(BF16)
    return high, low


def dot(left, right):
    return lax.dot_general(left, right, (((1,), (0,)), ((), ())), preferred_element_type=F32)


def table_left(table, values):
    high, low = parts(values)
    return dot(table[0], high) + dot(table[0], low) + dot(table[1], high)


def table_right(values, table, side):
    def times_table(piece, k):
        return lax.dot_general(
            piece, table[k], (((1,), (side,)), ((), ())), preferred_element_type=F32
        )

    high, low = parts(values)
    return times_table(high, 0) + times_table(low, 0) + times_table(high, 1)


def column(c):
    return slice(c * LN, (c + 1) * LN)


def forward(values, first, twist, second, work):
    grid = table_left(first, values)
    cosine, sine = twist[0], twist[1]
    for c in range(CH):
        real, imag = grid[:HALF, column(c)], grid[HALF:, column(c)]
        work[c * HALF : (c + 1) * HALF, :LN] = real * cosine + imag * sine
        work[c * HALF : (c + 1) * HALF, LN:] = imag * cosine - real * sine
    return table_right(work[...], second, 0)


def inverse(spectrum, twist, second, last):
    grid = table_right(spectrum, second, 1)
    cosine, sine = twist[0], twist[1]
    columns = []
    for c in range(CH):
        real = grid[c * HALF : (c + 1) * HALF, :LN]
        imag = grid[c * HALF : (c + 1) * HALF, LN:]
        columns.append(
            jnp.concatenate([real * cosine - imag * sine, imag * cosine + real * sine], axis=0)
        )
    return table_left(last, jnp.concatenate(columns, axis=1))


def times(first, second, conjugate):
    ar, ai = first[:, :LN], first[:, LN:]
    br, bi = second[:, :LN], second[:, LN:]
    if conjugate:
        return jnp.concatenate([ar * br + ai * bi, ar * bi - ai * br], axis=1)
    return jnp.concatenate([ar * br - ai * bi, ar * bi + ai * br], axis=1)


def lane_row():
    lane = lax.broadcasted_iota(jnp.int32, (SH, LN), 1)
    row = lax.broadcasted_iota(jnp.int32, (SH, LN), 0)
    return lane, row


def later(values, steps, lane, row):
    here = pltpu.roll(values, steps, 1)
    above = jnp.where(row >= 1, pltpu.roll(here, 1, 0), 0.0)
    return jnp.where(lane >= steps, here, above)


def sooner(values, steps, lane, row):
    here = pltpu.roll(values, LN - steps, 1)
    below = jnp.where(row < SH - 1, pltpu.roll(here, SH - 1, 0), 0.0)
    return jnp.where(lane < LN - steps, here, below)


def filter_kernel(filters, first, twist, second, spectrum, rows, work):
    for a in range(SH):
        rows[pl.ds(a, CH, stride=SH), :] = filters[:, column(a)]
    values = jnp.concatenate([rows[c * SH : (c + 1) * SH, :] for c in range(CH)], axis=1)
    spectrum[...] = forward(values, first, twist, second, work)


def front_kernel(
    streams, short_w, skip, kernel, first, twist, second, last,
    outgoing, query, left, right, signal, spectrum, rows, work, packed,
):
    lane, row = lane_row()
    for j in range(SH):
        rows[j * 48 : (j + 1) * 48, :] = streams[j].astype(F32)
    gated = []
    for c in range(CH):
        conv = []
        for s in range(3):
            x = rows[pl.ds(s * CH + c, SH, stride=48), :]
            y = short_w[s, 0, c] * x
            y = y + short_w[s, 1, c] * later(x, 1, lane, row)
            y = y + short_w[s, 2, c] * later(x, 2, lane, row)
            conv.append(y)
        query[:, column(c)] = conv[0].astype(BF16).astype(F32)
        left[:, column(c)] = conv[1]
        right[:, column(c)] = conv[2]
        gated.append((conv[1] * conv[2]).astype(BF16).astype(F32))
    own = forward(jnp.concatenate(gated, axis=1), first, twist, second, work)
    spectrum[...] = own
    total = inverse(times(kernel[...], own, False), twist, second, last)
    for c in range(CH):
        value = total[:, column(c)] + skip[c] * gated[c]
        signal[:, column(c)] = value
        packed[pl.ds(c, SH, stride=CH), :] = query[:, column(c)] * value
    for high in range(2):
        for low in range(4):
            for q in range(4):
                j = high * 16 + q * 4 + low
                piece = packed[j * CH : (j + 1) * CH, :].astype(BF16)
                for target in range(4):
                    outgoing[high * 16 + target * 4 + low, :, column(q)] = piece


def rear_kernel(
    upstream, short_w, skip, kernel, spectrum, query, left, right, signal,
    first, twist, second, last,
    outgoing, grad_filters, rows, work, packed, turned,
):
    lane, row = lane_row()
    for high in range(2):
        for low in range(4):
            total = upstream[high * 16 + low].astype(F32)
            for q in range(1, 4):
                total = total + upstream[high * 16 + q * 4 + low].astype(F32)
            for q in range(4):
                j = high * 16 + q * 4 + low
                rows[j * CH : (j + 1) * CH, :] = total[:, column(q)]

    def emit(s, c, x):
        y = short_w[s, 0, c] * x
        y = y + short_w[s, 1, c] * sooner(x, 1, lane, row)
        y = y + short_w[s, 2, c] * sooner(x, 2, lane, row)
        packed[pl.ds(s * CH + c, SH, stride=48), :] = y

    grad_signal = []
    for c in range(CH):
        up = rows[pl.ds(c, SH, stride=CH), :]
        grad_signal.append(up * query[:, column(c)])
        emit(0, c, (up * signal[:, column(c)]).astype(BF16).astype(F32))
    own = forward(jnp.concatenate(grad_signal, axis=1), first, twist, second, work)
    through = inverse(times(kernel[...], own, True), twist, second, last)
    for c in range(CH):
        grad = (through[:, column(c)] + skip[c] * grad_signal[c]).astype(BF16).astype(F32)
        emit(1, c, grad * right[:, column(c)])
        emit(2, c, grad * left[:, column(c)])
    for j in range(SH):
        outgoing[j] = packed[j * 48 : (j + 1) * 48, :].astype(BF16)
    taps = inverse(times(spectrum[...], own, True), twist, second, last)
    for c in range(CH):
        turned[c * SH : (c + 1) * SH, :] = taps[:, column(c)] * (SEQ**-0.5)
    for a in range(SH):
        grad_filters[:, column(a)] = turned[pl.ds(a, CH, stride=SH), :]


def weight_blocks(place, near, far, weight):
    for flip, blocks in ((0, near), (1, far)):
        for k in range(4):
            high = place[0] ^ (k >> 1)
            low = (place[1] ^ (k & 1)) * 2 + (place[2] ^ flip)
            weight[high, :, pl.ds(pl.multiple_of(low * LN, LN), LN)] = blocks[k]


def token_blocks(place, near, far, grad):
    for flip, blocks in ((0, near), (1, far)):
        for k in range(4):
            high = place[3] ^ (k >> 1)
            low = (place[4] ^ (k & 1)) * 2 + (place[5] ^ flip)
            grad[high, pl.ds(pl.multiple_of(low * LN, LN), LN), :] = blocks[k]


def product(left, right, over):
    return lax.dot_general(left, right, ((over[:1], over[1:]), ((), ())), preferred_element_type=F32)


def mixed_grad_kernel(place, w_near, w_far, g_near, g_far, _, outgoing, weight, grad):
    weight_blocks(place, w_near, w_far, weight)
    token_blocks(place, g_near, g_far, grad)
    for half in range(2):
        rows = slice(half * 256, (half + 1) * 256)
        total = product(weight[0, rows, :], grad[0], (1, 1))
        total = total + product(weight[1, rows, :], grad[1], (1, 1))
        outgoing[half * 16 : (half + 1) * 16] = total.astype(BF16).reshape(16, CH, 512)


def projection_kernel(
    place, mixed, w_near, w_far, g_near, g_far, o_near, o_far, d_near, d_far, weight, grad, held
):
    weight_blocks(place, w_near, w_far, weight)
    token_blocks(place, g_near, g_far, grad)
    rows = mixed[...].reshape(512, 512)
    for high in range(2):
        held[high] = product(rows, weight[high], (0, 0)).astype(BF16)
    for flip, blocks in ((0, o_near), (1, o_far)):
        for k in range(4):
            high = place[3] ^ (k >> 1)
            low = (place[4] ^ (k & 1)) * 2 + (place[5] ^ flip)
            blocks[k] = held[high, pl.ds(pl.multiple_of(low * LN, LN), LN), :]
    for high in range(2):
        held[high] = product(rows, grad[high], (1, 0)).astype(BF16)
    for flip, blocks in ((0, d_near), (1, d_far)):
        for k in range(4):
            high = place[0] ^ (k >> 1)
            low = (place[1] ^ (k & 1)) * 2 + (place[2] ^ flip)
            blocks[k] = held[high, :, pl.ds(pl.multiple_of(low * LN, LN), LN)]


def flat(*shape):
    return jax.ShapeDtypeStruct(shape, F32)


def half(*shape):
    return jax.ShapeDtypeStruct(shape, BF16)


def flip(values, axis, size, mask):
    return lax.ppermute(values, axis, [(i, i ^ mask) for i in range(size)])


def exchange(values):
    pairs = []
    for j in range(32):
        for i in range(8):
            to_j = (j & 0b10011) | ((i & 3) << 2)
            to_i = (i & 4) | ((j >> 2) & 3)
            pairs.append((j * 8 + i, to_j * 8 + to_i))
    return lax.ppermute(values, ("ctx", "tp"), pairs)


def shards(qkv, short_w, filters, skip, w_out, grad_out):
    first, twist, second, last = [jnp.asarray(t) for t in tables()]
    j, i = lax.axis_index("ctx"), lax.axis_index("tp")
    place = jnp.stack([j >> 4, (j >> 1) & 1, j & 1, i >> 2, (i >> 1) & 1, i & 1]).astype(jnp.int32)

    sent = qkv.reshape(3, SH, CH, LN).transpose(1, 0, 2, 3).reshape(SH, 3 * CH, LN)
    tile = exchange(grad_out)
    w_got = [flip(w_out, "ctx", 32, m) for m in (2, 16, 18)]
    sent, tile, place, *w_got = lax.optimization_barrier((sent, tile, place, *w_got))
    streams = lax.all_to_all(sent, "ctx", 0, 0)
    near = jnp.stack([tile] + [flip(tile, "tp", 8, m) for m in (2, 4, 6)])
    tiles = [near, flip(near, "tp", 8, 1)]
    w_near = jnp.stack([w_out, *w_got])
    w_far = flip(w_near, "ctx", 32, 1)

    kernel = pl.pallas_call(
        filter_kernel,
        out_shape=flat(CH * HALF, 2 * LN),
        in_specs=[VM] * 4,
        out_specs=VM,
        scratch_shapes=[pltpu.VMEM((CH * SH, LN), F32), pltpu.VMEM((CH * HALF, 2 * LN), F32)],
        compiler_params=PARAMS,
        name="filter_spectrum",
    )(filters, first, twist, second)

    buffer, query, left, right, signal, spectrum = pl.pallas_call(
        front_kernel,
        out_shape=[half(SH, 2 * CH, 512)] + [flat(SH, CH * LN)] * 4 + [flat(CH * HALF, 2 * LN)],
        in_specs=[VM, SM, SM] + [VM] * 5,
        out_specs=[pl.BlockSpec((SH, CH, 512), lambda g: (0, 0, 0))] + [VM] * 5,
        scratch_shapes=[
            pltpu.VMEM((SH * 48, LN), F32),
            pltpu.VMEM((CH * HALF, 2 * LN), F32),
            pltpu.VMEM((SH * CH, LN), F32),
        ],
        grid=(1,),
        compiler_params=PARAMS,
        name="front",
    )(streams, short_w, skip, kernel, first, twist, second, last)

    buffer = pl.pallas_call(
        mixed_grad_kernel,
        out_shape=half(SH, 2 * CH, 512),
        in_specs=[SM] + [VM] * 4 + [pl.BlockSpec(memory_space=pl.ANY)],
        out_specs=pl.BlockSpec((SH, CH, 512), lambda g: (0, 1, 0)),
        scratch_shapes=[pltpu.VMEM((2, 512, 512), BF16), pltpu.VMEM((2, 512, 512), BF16)],
        input_output_aliases={5: 0},
        grid=(1,),
        compiler_params=PARAMS,
        name="mixed_grad",
    )(place, w_near, w_far, *tiles, buffer)

    joint = lax.all_to_all(buffer, "ctx", 0, 0)

    o_near, o_far, d_near, d_far = pl.pallas_call(
        projection_kernel,
        out_shape=[half(4, LN, 512)] * 2 + [half(4, 512, LN)] * 2,
        in_specs=[SM, pl.BlockSpec((SH, CH, 512), lambda g: (0, 0, 0))] + [VM] * 4,
        out_specs=[VM] * 4,
        scratch_shapes=[pltpu.VMEM((2, 512, 512), BF16)] * 3,
        grid=(1,),
        compiler_params=PARAMS,
        name="projections",
    )(place, joint, w_near, w_far, *tiles)

    o_sum = o_near.astype(F32) + flip(o_far, "tp", 8, 1).astype(F32)
    o_sent = o_sum.astype(BF16)
    o_total = o_sent[0].astype(F32)
    for k in range(1, 4):
        o_total = o_total + flip(o_sent[k], "tp", 8, 2 * k).astype(F32)
    output = exchange(o_total.astype(BF16))

    d_sum = (d_near.astype(F32) + flip(d_far, "ctx", 32, 1).astype(F32)).astype(BF16)
    d_total = d_sum[0].astype(F32)
    for k, m in ((1, 2), (2, 16), (3, 18)):
        d_total = d_total + flip(d_sum[k], "ctx", 32, m).astype(F32)
    grad_w_out = d_total * (SEQ**-0.5)

    grads, grad_filters = pl.pallas_call(
        rear_kernel,
        out_shape=[half(SH, 3 * CH, LN), flat(CH, SEQ)],
        in_specs=[pl.BlockSpec((SH, CH, 512), lambda g: (0, 1, 0)), SM, SM] + [VM] * 10,
        out_specs=[VM, VM],
        scratch_shapes=[
            pltpu.VMEM((SH * CH, LN), F32),
            pltpu.VMEM((CH * HALF, 2 * LN), F32),
            pltpu.VMEM((SH * 48, LN), F32),
            pltpu.VMEM((CH * SH, LN), F32),
        ],
        grid=(1,),
        compiler_params=PARAMS,
        name="rear",
    )(joint, short_w, skip, kernel, spectrum, query, left, right, signal, first, twist, second, last)

    returned = lax.all_to_all(grads, "ctx", 0, 0)
    grad_qkv = returned.reshape(SH, 3, CH, LN).transpose(1, 0, 2, 3).reshape(3, SH * CH, LN)
    return (output, grad_qkv, grad_filters, grad_w_out)


def solution(mesh):
    placed = (
        P(None, "tp", "ctx"),
        P(None, None, ("tp", "ctx")),
        P(("tp", "ctx"), None),
        P(("tp", "ctx")),
        P("tp", "ctx"),
        P("ctx", "tp"),
    )
    return jax.shard_map(
        shards,
        mesh=mesh,
        in_specs=placed,
        out_specs=(P("ctx", "tp"), P(None, "tp", "ctx"), P(("tp", "ctx"), None), P("tp", "ctx")),
        check_vma=False,
    )
```

```python
import functools
import math

import jax
import jax.numpy as jnp
import ml_dtypes
import numpy as np
from jax import lax
from jax.experimental import pallas as pl
from jax.experimental.pallas import tpu as pltpu
from jax.sharding import PartitionSpec as P

F32 = jnp.float32
BF16 = jnp.bfloat16
SEQ = 4096
CH = 16
SH = 32
LN = 128
HALF = 40
VM = pl.BlockSpec(memory_space=pltpu.VMEM)
SM = pl.BlockSpec(memory_space=pltpu.SMEM)
PARAMS = pltpu.CompilerParams(vmem_limit_bytes=32 * 1024 * 1024)


def split(table):
    high = table.astype(ml_dtypes.bfloat16)
    low = (table - high.astype(np.float64)).astype(ml_dtypes.bfloat16)
    return np.stack([high, low])


def tables():
    d = np.arange(HALF)[:, None]
    live = d <= 32
    a = np.arange(SH)[None, :]
    b = np.arange(LN)
    one = 2 * math.pi * d * a / 64
    first = np.concatenate([np.cos(one) * live, -np.sin(one) * live], axis=0)
    turn = 2 * math.pi * d * b[None, :] / 8192
    twist = np.stack([np.cos(turn), np.sin(turn)]).astype(np.float32)
    two = 2 * math.pi * b[:, None] * b[None, :] / 128
    c2, s2 = np.cos(two), np.sin(two)
    second = np.block([[c2, -s2], [s2, c2]])
    weight = np.where((d == 0) | (d == 32), 1.0, 2.0) * live / 8192
    last = np.concatenate([(np.cos(one) * weight).T, (-np.sin(one) * weight).T], axis=1)
    return split(first), twist, split(second), split(last)


def parts(values):
    high = values.astype(BF16)
    low = (values - high.astype(F32)).astype(BF16)
    return high, low


def dot(left, right):
    return lax.dot_general(left, right, (((1,), (0,)), ((), ())), preferred_element_type=F32)


def table_left(table, values):
    high, low = parts(values)
    return dot(table[0], high) + dot(table[0], low) + dot(table[1], high)


def table_right(values, table, side):
    def times_table(piece, k):
        return lax.dot_general(
            piece, table[k], (((1,), (side,)), ((), ())), preferred_element_type=F32
        )

    high, low = parts(values)
    return times_table(high, 0) + times_table(low, 0) + times_table(high, 1)


def column(c):
    return slice(c * LN, (c + 1) * LN)


def forward(values, first, twist, second, work):
    grid = table_left(first, values)
    cosine, sine = twist[0], twist[1]
    for c in range(CH):
        real, imag = grid[:HALF, column(c)], grid[HALF:, column(c)]
        work[c * HALF : (c + 1) * HALF, :LN] = real * cosine + imag * sine
        work[c * HALF : (c + 1) * HALF, LN:] = imag * cosine - real * sine
    return table_right(work[...], second, 0)


def inverse(spectrum, twist, second, last):
    grid = table_right(spectrum, second, 1)
    cosine, sine = twist[0], twist[1]
    columns = []
    for c in range(CH):
        real = grid[c * HALF : (c + 1) * HALF, :LN]
        imag = grid[c * HALF : (c + 1) * HALF, LN:]
        columns.append(
            jnp.concatenate([real * cosine - imag * sine, imag * cosine + real * sine], axis=0)
        )
    return table_left(last, jnp.concatenate(columns, axis=1))


def times(first, second, conjugate):
    ar, ai = first[:, :LN], first[:, LN:]
    br, bi = second[:, :LN], second[:, LN:]
    if conjugate:
        return jnp.concatenate([ar * br + ai * bi, ar * bi - ai * br], axis=1)
    return jnp.concatenate([ar * br - ai * bi, ar * bi + ai * br], axis=1)


def lane_row():
    lane = lax.broadcasted_iota(jnp.int32, (SH, LN), 1)
    row = lax.broadcasted_iota(jnp.int32, (SH, LN), 0)
    return lane, row


def later(values, steps, lane, row):
    here = pltpu.roll(values, steps, 1)
    above = jnp.where(row >= 1, pltpu.roll(here, 1, 0), 0.0)
    return jnp.where(lane >= steps, here, above)


def sooner(values, steps, lane, row):
    here = pltpu.roll(values, LN - steps, 1)
    below = jnp.where(row < SH - 1, pltpu.roll(here, SH - 1, 0), 0.0)
    return jnp.where(lane < LN - steps, here, below)


def filter_kernel(filters, first, twist, second, spectrum, rows, work):
    for a in range(SH):
        rows[pl.ds(a, CH, stride=SH), :] = filters[:, column(a)]
    values = jnp.concatenate([rows[c * SH : (c + 1) * SH, :] for c in range(CH)], axis=1)
    spectrum[...] = forward(values, first, twist, second, work)


def front_kernel(
    streams, short_w, skip, kernel, first, twist, second, last,
    outgoing, query, left, right, signal, spectrum, rows, work, packed,
):
    lane, row = lane_row()
    for j in range(SH):
        rows[j * 48 : (j + 1) * 48, :] = streams[j].astype(F32)
    gated = []
    for c in range(CH):
        conv = []
        for s in range(3):
            x = rows[pl.ds(s * CH + c, SH, stride=48), :]
            y = short_w[s, 0, c] * x
            y = y + short_w[s, 1, c] * later(x, 1, lane, row)
            y = y + short_w[s, 2, c] * later(x, 2, lane, row)
            conv.append(y)
        query[:, column(c)] = conv[0].astype(BF16).astype(F32)
        left[:, column(c)] = conv[1]
        right[:, column(c)] = conv[2]
        gated.append((conv[1] * conv[2]).astype(BF16).astype(F32))
    own = forward(jnp.concatenate(gated, axis=1), first, twist, second, work)
    spectrum[...] = own
    total = inverse(times(kernel[...], own, False), twist, second, last)
    for c in range(CH):
        value = total[:, column(c)] + skip[c] * gated[c]
        signal[:, column(c)] = value
        packed[pl.ds(c, SH, stride=CH), :] = query[:, column(c)] * value
    for high in range(2):
        for low in range(4):
            for q in range(4):
                j = high * 16 + q * 4 + low
                piece = packed[j * CH : (j + 1) * CH, :].astype(BF16)
                for target in range(4):
                    outgoing[high * 16 + target * 4 + low, :, column(q)] = piece


def rear_kernel(
    upstream, short_w, skip, kernel, spectrum, query, left, right, signal,
    first, twist, second, last,
    outgoing, grad_filters, rows, work, packed, turned,
):
    lane, row = lane_row()
    for high in range(2):
        for low in range(4):
            total = upstream[high * 16 + low].astype(F32)
            for q in range(1, 4):
                total = total + upstream[high * 16 + q * 4 + low].astype(F32)
            for q in range(4):
                j = high * 16 + q * 4 + low
                rows[j * CH : (j + 1) * CH, :] = total[:, column(q)]

    def emit(s, c, x):
        y = short_w[s, 0, c] * x
        y = y + short_w[s, 1, c] * sooner(x, 1, lane, row)
        y = y + short_w[s, 2, c] * sooner(x, 2, lane, row)
        packed[pl.ds(s * CH + c, SH, stride=48), :] = y

    grad_signal = []
    for c in range(CH):
        up = rows[pl.ds(c, SH, stride=CH), :]
        grad_signal.append(up * query[:, column(c)])
        emit(0, c, (up * signal[:, column(c)]).astype(BF16).astype(F32))
    own = forward(jnp.concatenate(grad_signal, axis=1), first, twist, second, work)
    through = inverse(times(kernel[...], own, True), twist, second, last)
    for c in range(CH):
        grad = (through[:, column(c)] + skip[c] * grad_signal[c]).astype(BF16).astype(F32)
        emit(1, c, grad * right[:, column(c)])
        emit(2, c, grad * left[:, column(c)])
    for j in range(SH):
        outgoing[j] = packed[j * 48 : (j + 1) * 48, :].astype(BF16)
    taps = inverse(times(spectrum[...], own, True), twist, second, last)
    for c in range(CH):
        turned[c * SH : (c + 1) * SH, :] = taps[:, column(c)] * (SEQ**-0.5)
    for a in range(SH):
        grad_filters[:, column(a)] = turned[pl.ds(a, CH, stride=SH), :]


def weight_blocks(place, near, far, weight):
    for flip, blocks in ((0, near), (1, far)):
        for k in range(4):
            high = place[0] ^ (k >> 1)
            low = (place[1] ^ (k & 1)) * 2 + (place[2] ^ flip)
            weight[high, :, pl.ds(pl.multiple_of(low * LN, LN), LN)] = blocks[k]


def token_blocks(place, near, far, grad):
    for flip, blocks in ((0, near), (1, far)):
        for k in range(4):
            high = place[3] ^ (k >> 1)
            low = (place[4] ^ (k & 1)) * 2 + (place[5] ^ flip)
            grad[high, pl.ds(pl.multiple_of(low * LN, LN), LN), :] = blocks[k]


def product(left, right, over):
    return lax.dot_general(left, right, ((over[:1], over[1:]), ((), ())), preferred_element_type=F32)


def mixed_grad_kernel(place, w_near, w_far, g_near, g_far, _, outgoing, weight, grad):
    weight_blocks(place, w_near, w_far, weight)
    token_blocks(place, g_near, g_far, grad)
    for half in range(2):
        rows = slice(half * 256, (half + 1) * 256)
        total = product(weight[0, rows, :], grad[0], (1, 1))
        total = total + product(weight[1, rows, :], grad[1], (1, 1))
        outgoing[half * 16 : (half + 1) * 16] = total.astype(BF16).reshape(16, CH, 512)


def projection_kernel(
    place, mixed, w_near, w_far, g_near, g_far, o_near, o_far, d_near, d_far, weight, grad, held
):
    weight_blocks(place, w_near, w_far, weight)
    token_blocks(place, g_near, g_far, grad)
    rows = mixed[...].reshape(512, 512)
    for high in range(2):
        held[high] = product(rows, weight[high], (0, 0)).astype(BF16)
    for flip, blocks in ((0, o_near), (1, o_far)):
        for k in range(4):
            high = place[3] ^ (k >> 1)
            low = (place[4] ^ (k & 1)) * 2 + (place[5] ^ flip)
            blocks[k] = held[high, pl.ds(pl.multiple_of(low * LN, LN), LN), :]
    for high in range(2):
        held[high] = product(rows, grad[high], (1, 0)).astype(BF16)
    for flip, blocks in ((0, d_near), (1, d_far)):
        for k in range(4):
            high = place[0] ^ (k >> 1)
            low = (place[1] ^ (k & 1)) * 2 + (place[2] ^ flip)
            blocks[k] = held[high, :, pl.ds(pl.multiple_of(low * LN, LN), LN)]


def flat(*shape):
    return jax.ShapeDtypeStruct(shape, F32)


def half(*shape):
    return jax.ShapeDtypeStruct(shape, BF16)


def flip(values, axis, size, mask):
    return lax.ppermute(values, axis, [(i, i ^ mask) for i in range(size)])


def exchange(values):
    pairs = []
    for j in range(32):
        for i in range(8):
            to_j = (j & 0b10011) | ((i & 3) << 2)
            to_i = (i & 4) | ((j >> 2) & 3)
            pairs.append((j * 8 + i, to_j * 8 + to_i))
    return lax.ppermute(values, ("ctx", "tp"), pairs)


def shards(qkv, short_w, filters, skip, w_out, grad_out):
    first, twist, second, last = [jnp.asarray(t) for t in tables()]
    j, i = lax.axis_index("ctx"), lax.axis_index("tp")
    place = jnp.stack([j >> 4, (j >> 1) & 1, j & 1, i >> 2, (i >> 1) & 1, i & 1]).astype(jnp.int32)

    sent = qkv.reshape(3, SH, CH, LN).transpose(1, 0, 2, 3).reshape(SH, 3 * CH, LN)
    tile = exchange(grad_out)
    w_got = [flip(w_out, "ctx", 32, m) for m in (2, 16, 18)]
    sent, tile, place, *w_got = lax.optimization_barrier((sent, tile, place, *w_got))
    streams = lax.all_to_all(sent, "ctx", 0, 0)
    near = jnp.stack([tile] + [flip(tile, "tp", 8, m) for m in (2, 4, 6)])
    tiles = [near, flip(near, "tp", 8, 1)]
    w_near = jnp.stack([w_out, *w_got])
    streams, _ = lax.optimization_barrier((streams, near))
    w_far = flip(w_near, "ctx", 32, 1)

    kernel = pl.pallas_call(
        filter_kernel,
        out_shape=flat(CH * HALF, 2 * LN),
        in_specs=[VM] * 4,
        out_specs=VM,
        scratch_shapes=[pltpu.VMEM((CH * SH, LN), F32), pltpu.VMEM((CH * HALF, 2 * LN), F32)],
        compiler_params=PARAMS,
        name="filter_spectrum",
    )(filters, first, twist, second)

    buffer, query, left, right, signal, spectrum = pl.pallas_call(
        front_kernel,
        out_shape=[half(SH, 2 * CH, 512)] + [flat(SH, CH * LN)] * 4 + [flat(CH * HALF, 2 * LN)],
        in_specs=[VM, SM, SM] + [VM] * 5,
        out_specs=[pl.BlockSpec((SH, CH, 512), lambda g: (0, 0, 0))] + [VM] * 5,
        scratch_shapes=[
            pltpu.VMEM((SH * 48, LN), F32),
            pltpu.VMEM((CH * HALF, 2 * LN), F32),
            pltpu.VMEM((SH * CH, LN), F32),
        ],
        grid=(1,),
        compiler_params=PARAMS,
        name="front",
    )(streams, short_w, skip, kernel, first, twist, second, last)

    buffer = pl.pallas_call(
        mixed_grad_kernel,
        out_shape=half(SH, 2 * CH, 512),
        in_specs=[SM] + [VM] * 4 + [pl.BlockSpec(memory_space=pl.ANY)],
        out_specs=pl.BlockSpec((SH, CH, 512), lambda g: (0, 1, 0)),
        scratch_shapes=[pltpu.VMEM((2, 512, 512), BF16), pltpu.VMEM((2, 512, 512), BF16)],
        input_output_aliases={5: 0},
        grid=(1,),
        compiler_params=PARAMS,
        name="mixed_grad",
    )(place, w_near, w_far, *tiles, buffer)

    joint = lax.all_to_all(buffer, "ctx", 0, 0)

    o_near, o_far, d_near, d_far = pl.pallas_call(
        projection_kernel,
        out_shape=[half(4, LN, 512)] * 2 + [half(4, 512, LN)] * 2,
        in_specs=[SM, pl.BlockSpec((SH, CH, 512), lambda g: (0, 0, 0))] + [VM] * 4,
        out_specs=[VM] * 4,
        scratch_shapes=[pltpu.VMEM((2, 512, 512), BF16)] * 3,
        grid=(1,),
        compiler_params=PARAMS,
        name="projections",
    )(place, joint, w_near, w_far, *tiles)

    o_sum = o_near.astype(F32) + flip(o_far, "tp", 8, 1).astype(F32)
    o_sent = o_sum.astype(BF16)
    o_total = o_sum[0]
    for k in range(1, 4):
        o_total = o_total + flip(o_sent[k], "tp", 8, 2 * k).astype(F32)
    output = exchange(o_total.astype(BF16))

    d_sum = d_near.astype(F32) + flip(d_far, "ctx", 32, 1).astype(F32)
    d_sent = d_sum.astype(BF16)
    d_total = d_sum[0]
    for k, m in ((1, 2), (2, 16), (3, 18)):
        d_total = d_total + flip(d_sent[k], "ctx", 32, m).astype(F32)
    grad_w_out = d_total * (SEQ**-0.5)

    grads, grad_filters = pl.pallas_call(
        rear_kernel,
        out_shape=[half(SH, 3 * CH, LN), flat(CH, SEQ)],
        in_specs=[pl.BlockSpec((SH, CH, 512), lambda g: (0, 1, 0)), SM, SM] + [VM] * 10,
        out_specs=[VM, VM],
        scratch_shapes=[
            pltpu.VMEM((SH * CH, LN), F32),
            pltpu.VMEM((CH * HALF, 2 * LN), F32),
            pltpu.VMEM((SH * 48, LN), F32),
            pltpu.VMEM((CH * SH, LN), F32),
        ],
        grid=(1,),
        compiler_params=PARAMS,
        name="rear",
    )(joint, short_w, skip, kernel, spectrum, query, left, right, signal, first, twist, second, last)

    returned = lax.all_to_all(grads, "ctx", 0, 0)
    grad_qkv = returned.reshape(SH, 3, CH, LN).transpose(1, 0, 2, 3).reshape(3, SH * CH, LN)
    return (output, grad_qkv, grad_filters, grad_w_out)


def solution(mesh):
    placed = (
        P(None, "tp", "ctx"),
        P(None, None, ("tp", "ctx")),
        P(("tp", "ctx"), None),
        P(("tp", "ctx")),
        P("tp", "ctx"),
        P("ctx", "tp"),
    )
    return jax.shard_map(
        shards,
        mesh=mesh,
        in_specs=placed,
        out_specs=(P("ctx", "tp"), P(None, "tp", "ctx"), P(("tp", "ctx"), None), P("tp", "ctx")),
        check_vma=False,
    )
```
